256 devices in a mesh: tm: 64 (over z, x, core), space: 4 (over y).
Axes of the slice: x: 4, y: 4, z: 8, core: 2. Of those that a mesh axis runs over, the one named last changes fastest.
Arguments:
- states: float32 [64, 2, 64, 256], P('tm', None, 'space'), may hold values from -6 to 6
- vel_x: int32 [64, 256], replicated, may hold values from -15 to 15
- vel_y: int32 [64, 256], replicated, may hold values from -15 to 15
- diffus: int32 [64, 256], replicated, may hold values from 1 to 10
Outputs:
- corrected: float32 [64, 2, 64, 256], P('tm', None, 'space')
- advanced: float32 [64, 2, 64, 256], P('tm', None, 'space')
- residual: float32 [64, 2, 64, 256], P('tm', None, 'space')
The draws below stay inside these ranges and needn't reach their ends.
All inputs are finite; a program needn't handle non-finite values.
Results may differ from the reference program's by a relative error of at most 0.00002.
Values sent between devices are 32-bit elements; how exact they have to be, the bound alone decides.
No kernel may reach another device: no remote copies, remote signals or barrier semaphores. Data moves between devices by JAX's collectives and lax.ppermute only.
A program may use at most 64 MiB of HBM per device.

```python
import jax
import jax.numpy as jnp
from jax import lax

COLS = 256
STEPS = 16
NX = 64
INTERVALS = 64


def plant(values, stream_key, smallest, largest):
    spot = [jax.random.randint(jax.random.fold_in(stream_key, axis), (), 0, length) for axis, length in enumerate(values.shape)]
    main_axis = values.shape.index(max(values.shape))
    neighbour = spot[:main_axis] + [(spot[main_axis] + 1) % values.shape[main_axis]] + spot[main_axis + 1:]
    return values.at[tuple(spot)].set(smallest).at[tuple(neighbour)].set(largest)


def block_scale(rng, shape, split, low, largest):
    gain, own = 1.0, jax.random.fold_in(rng, 6)
    for axis_at, shards_of in split:
        draws = jnp.exp(jax.random.uniform(jax.random.fold_in(own, axis_at), (shards_of,), jnp.float32, low / len(split), largest / len(split)))
        gain = gain * jnp.repeat(draws, shape[axis_at] // shards_of).reshape([-1 if axis == axis_at else 1 for axis in range(len(shape))])
    return gain


def noise(rng, extent, deviation, reach, shards=(), held_as=jnp.bfloat16):
    drawn = deviation * jax.random.normal(rng, extent, jnp.float32)
    if shards:
        drawn = drawn * block_scale(rng, extent, shards, -0.22, 0.18)
    return jnp.clip(drawn, -reach, reach).astype(held_as)


def setup_inputs(seed: int = 0) -> dict:
    arg_keys = jax.random.split(jax.random.key(seed), 5)
    return {
        "states": noise(arg_keys[0], (INTERVALS, 2, NX, COLS), 1.0, 6.0, ((0, 64), (2, 4)), jnp.float32),
        "vel_x": plant(jax.random.randint(arg_keys[1], (NX, COLS), -15, 16), jax.random.fold_in(arg_keys[1], 1), -15, 15).astype(jnp.int32),
        "vel_y": plant(jax.random.randint(arg_keys[2], (NX, COLS), -15, 16), jax.random.fold_in(arg_keys[2], 1), -15, 15).astype(jnp.int32),
        "diffus": plant(jax.random.randint(arg_keys[3], (NX, COLS), 1, 11), jax.random.fold_in(arg_keys[3], 1), 1, 10).astype(jnp.int32),
    }


def tracer_scales():
    return jnp.array([1.0, 0.5], jnp.float32)[:, None, None]


def coefficients(vel_x, vel_y, diffus):
    return (0.01 * vel_x.astype(jnp.float32), 0.01 * vel_y.astype(jnp.float32), 0.005 * diffus.astype(jnp.float32))


def advance(field, coefs, factor):
    courant_x, courant_y, diffusion = coefs
    widths = ((0, 0),) * (field.ndim - 2) + ((1, 1), (1, 1))
    padded = jnp.pad(field, widths)
    row_above = padded[..., :-2, 1:-1]
    row_below = padded[..., 2:, 1:-1]
    column_left = padded[..., 1:-1, :-2]
    column_right = padded[..., 1:-1, 2:]
    transport = (jnp.maximum(courant_x, 0.0) * (field - row_above) + jnp.minimum(courant_x, 0.0) * (row_below - field)
                 + jnp.maximum(courant_y, 0.0) * (field - column_left) + jnp.minimum(courant_y, 0.0) * (column_right - field))
    laplace = row_above + row_below + column_left + column_right - 4.0 * field
    return field + factor * (diffusion * tracer_scales() * laplace - transport)


def propagate(field, count, factor, coefs):
    return lax.fori_loop(0, count, lambda turn_index, current: advance(current, coefs, factor), field)


def reference(states, vel_x, vel_y, diffus):
    coefs = coefficients(vel_x, vel_y, diffus)
    interval_ends = propagate(states, STEPS, 1.0, coefs)
    starts = jnp.concatenate([states[:1], interval_ends[:-1]], 0)
    second_ends = propagate(starts, STEPS, 1.0, coefs)
    coarse_starts = propagate(starts, STEPS // 2, 2.0, coefs)
    residual = jnp.concatenate([jnp.zeros_like(states[:1]), second_ends[:-1] - starts[1:]], 0)
    forcing = jnp.concatenate([states[:1], second_ends[:-1] - coarse_starts[:-1]], 0)

    def coarse_turn(carried, forcing_slot):
        updated = propagate(carried, STEPS // 2, 2.0, coefs) + forcing_slot
        return updated, updated

    _, corrected = lax.scan(coarse_turn, jnp.zeros(states.shape[1:], jnp.float32), forcing)
    advanced = propagate(corrected, STEPS, 1.0, coefs)
    return corrected, advanced, residual
```

```python
import functools

import jax
import jax.numpy as jnp
import numpy as np
from jax import lax
from jax.experimental import pallas as pl
from jax.experimental.pallas import tpu as pltpu
from jax.sharding import Mesh
from jax.sharding import PartitionSpec as P

STEPS = 16
ROWS, COLS = 64, 256
PLANES, PLACES, PARTS = 8, 8, 4
INTERVALS = PLANES * PLACES
TILES = 16
VMEM = pl.BlockSpec(memory_space=pltpu.VMEM)
F32, BF16 = jnp.float32, jnp.bfloat16


def diamond(radius):
    reach = range(-radius, radius + 1)
    return [(dr, dc) for dr in reach for dc in reach if abs(dr) + abs(dc) <= radius]


class Shifted:
    def __init__(self, tiles):
        self.tiles, self.made = tiles, {}

    def at(self, i, column):
        lanes, j = divmod(column, 2)
        key = (i, j, lanes)
        if key not in self.made:
            if not 0 <= i < 8:
                self.made[key] = pltpu.roll(self.at(i % 8, column), 1 if i < 0 else 7, 0)
            elif lanes:
                self.made[key] = pltpu.roll(self.tiles[2 * i + j], (-lanes) % 128, 1)
            else:
                self.made[key] = self.tiles[2 * i + j]
        return self.made[key]


def apply(tiles, coef, radius):
    moved, points, result = Shifted(tiles), diamond(radius), []
    for i in range(8):
        for j in range(2):
            order = sorted(range(len(points)), key=lambda n: (abs((j + points[n][1]) // 2), points[n][1], points[n][0]))
            total = None
            for n in order:
                term = coef[n, 2 * i + j] * moved.at(i + points[n][0], j + points[n][1])
                total = term if total is None else total + term
            result.append(total)
    return tuple(result)


def five_point(levels, tracer, factor, out):
    lane = lax.broadcasted_iota(jnp.int32, (8, 128), 1)
    sublane = lax.broadcasted_iota(jnp.int32, (8, 128), 0)
    scale = jnp.where(tracer == 0, 1.0, 0.5).astype(F32)
    offsets = diamond(1)
    for i in range(8):
        for j in range(2):
            k = 2 * i + j
            courant_x, courant_y = 0.01 * levels[0, k], 0.01 * levels[1, k]
            spread = scale * (0.005 * levels[2, k])
            above = factor * (spread + jnp.maximum(courant_x, 0.0))
            below = factor * (spread - jnp.minimum(courant_x, 0.0))
            left = factor * (spread + jnp.maximum(courant_y, 0.0))
            right = factor * (spread - jnp.minimum(courant_y, 0.0))
            middle = 1.0 - factor * (4.0 * spread + jnp.abs(courant_x) + jnp.abs(courant_y))
            if i == 0:
                above = jnp.where(sublane == 0, 0.0, above)
            if i == 7:
                below = jnp.where(sublane == 7, 0.0, below)
            if j == 0:
                left = jnp.where(lane == 0, 0.0, left)
            if j == 1:
                right = jnp.where(lane == 127, 0.0, right)
            for offset, value in (((0, 0), middle), ((-1, 0), above), ((1, 0), below), ((0, -1), left), ((0, 1), right)):
                out[offsets.index(offset), k] = value


def compose(one, source, radius, out):
    near, old = diamond(1), diamond(radius)
    for n, (row, column) in enumerate(diamond(radius + 1)):
        totals = [None] * TILES
        for m, (dr, dc) in enumerate(near):
            if (row - dr, column - dc) not in old:
                continue
            at = old.index((row - dr, column - dc))
            moved = Shifted([source[at, k] for k in range(TILES)])
            for k in range(TILES):
                term = one[m, k] * moved.at(k // 2 + dr, k % 2 + dc)
                totals[k] = term if totals[k] is None else totals[k] + term
        for k in range(TILES):
            out[n, k] = totals[k]


def coef_scratch(radius):
    return pltpu.VMEM((len(diamond(radius)), TILES, 8, 128), F32)


def load_flat(ref, start=0):
    return tuple(ref[pl.ds(start + 2 * i + j, 8, stride=16), :] for i in range(8) for j in range(2))


def store_flat(ref, tiles):
    for i in range(8):
        for j in range(2):
            ref[pl.ds(2 * i + j, 8, stride=16), :] = tiles[2 * i + j]


def load_tiles(ref, *at):
    return tuple(ref[(*at, k)] for k in range(TILES))


def store_tiles(ref, tiles, *at):
    for k in range(TILES):
        ref[(*at, k)] = tiles[k]


def added(a, b):
    return tuple(x + y for x, y in zip(a, b, strict=True))


def split_matrix(back):
    row = lax.broadcasted_iota(jnp.int32, (COLS, COLS), 0)
    column = lax.broadcasted_iota(jnp.int32, (COLS, COLS), 1)
    if back:
        row, column = column, row
    return jnp.where(row == 2 * (column % 128) + column // 128, 1.0, 0.0).astype(BF16)


def permuted(x, matrix):
    high = x.astype(BF16)
    rest = x - high.astype(F32)
    middle = rest.astype(BF16)
    low = (rest - middle.astype(F32)).astype(BF16)
    dot = functools.partial(jnp.dot, preferred_element_type=F32)
    return (dot(high, matrix) + dot(middle, matrix)) + dot(low, matrix)


def prepare_kernel(states, out):
    both = jnp.concatenate([states[0, 0], states[0, 1]], 0)
    moved = permuted(both, split_matrix(False))
    for part in range(PARTS):
        rows = moved[16 * (part // 2) : 16 * (part // 2) + 16]
        for j in range(2):
            out[part, pl.ds(j, 16, stride=2), :] = rows[:, 128 * j : 128 * j + 128]


def own_kernel(whole, vel_x, vel_y, diffus, levels, carried, forcing, stage, fine1, coarse1, fine2, coarse2):
    interval = lax.axis_index("z") * PLACES + lax.axis_index("place")
    tracer = lax.axis_index("space") // 2
    matrix = split_matrix(False)
    for n, table in enumerate((vel_x, vel_y, diffus)):
        moved = jnp.dot(table[...].astype(F32).astype(BF16), matrix, preferred_element_type=F32)
        for j in range(2):
            stage[pl.ds(j, ROWS, stride=2), :] = moved[:, 128 * j : 128 * j + 128]
        store_tiles(levels, load_flat(stage), n)
    five_point(levels, tracer, 1.0, fine1)
    five_point(levels, tracer, 2.0, coarse1)
    compose(fine1, fine1, 1, fine2)
    compose(coarse1, coarse1, 1, coarse2)
    start = load_flat(whole)

    def body(_, fields):
        ahead, image = fields
        image = apply(image, coarse2, 2)
        ahead = apply(apply(ahead, fine2, 2), fine2, 2)
        return ahead, image

    ahead, image = lax.fori_loop(0, STEPS // 4, body, (start, start))
    store_tiles(carried, ahead)
    first = interval == 0
    for k in range(TILES):
        value = jnp.where(first, ahead[k], ahead[k] - image[k])
        for plane in range(PLANES):
            forcing[plane, k] = value


def coarse_interval(tiles, coarse2, coarse3):
    return apply(apply(apply(tiles, coarse3, 3), coarse3, 3), coarse2, 2)


def planes_kernel(forcings, levels, out, before, coarse1, coarse2, coarse3):
    plane, place = lax.axis_index("z"), lax.axis_index("place")
    tracer = lax.axis_index("space") // 2
    five_point(levels, tracer, 2.0, coarse1)
    compose(coarse1, coarse1, 1, coarse2)
    compose(coarse1, coarse2, 2, coarse3)
    store_tiles(before, tuple(jnp.zeros((8, 128), F32) for _ in range(TILES)))

    def one_plane(b, tiles):
        store_tiles(before, tiles)
        tiles = lax.fori_loop(0, PLACES, lambda _, now: coarse_interval(now, coarse2, coarse3), tiles)
        return added(tiles, load_tiles(forcings, b))

    total = lax.fori_loop(1, plane + 1, one_plane, load_tiles(forcings, 0))
    spare = (plane == PLANES - 1) & (place == 0)
    for target in range(PLACES):
        for k in range(TILES):
            value = jnp.where(place <= target, total[k], before[k])
            if target >= PLACES - 2:
                value = jnp.where(spare, forcings[0, k], value)
            out[target, k] = value


def finish_kernel(sums, following, carried, levels, out_a, out_b, corrected, left, stage, fine1, fine2, coarse1, coarse2, coarse3):
    plane, place, part = lax.axis_index("z"), lax.axis_index("place"), lax.axis_index("space")
    interval = plane * PLACES + place
    tracer = part // 2
    five_point(levels, tracer, 2.0, coarse1)
    compose(coarse1, coarse1, 1, coarse2)
    compose(coarse1, coarse2, 2, coarse3)
    five_point(levels, tracer, 1.0, fine1)
    compose(fine1, fine1, 1, fine2)

    def neighbour(k, tiles):
        at = lax.rem(place + 1 + k, PLACES)
        return added(coarse_interval(tiles, coarse2, coarse3), load_tiles(sums, at))

    total = lax.fori_loop(1, PLACES, neighbour, load_tiles(sums, lax.rem(place + 1, PLACES)))
    total = lax.fori_loop(0, STEPS // 2, lambda _, now: apply(now, fine2, 2), total)
    given = load_tiles(sums, 0)
    total = tuple(jnp.where(interval >= INTERVALS - 2, g, t) for g, t in zip(given, total, strict=True))
    store_tiles(corrected, total)
    gap = tuple(c - n for c, n in zip(load_tiles(carried), load_flat(following), strict=True))

    def body(_, fields):
        return tuple(apply(field, fine2, 2) for field in fields)

    advanced, residual = lax.fori_loop(0, STEPS // 2, body, (total, gap))
    advanced = tuple(jnp.where(interval == INTERVALS - 2, g, a) for g, a in zip(load_tiles(sums, 0), advanced, strict=True))
    to_a = 2 * lax.rem(part, 2) + part // 2
    to_b = 2 * lax.rem(part, 2) + 1 - part // 2
    for n, tiles in enumerate((load_tiles(corrected), advanced, residual)):
        store_flat(stage, tiles)
        out_a[pl.ds(32 * n, 32), :] = stage[pl.ds(pl.multiple_of(32 * to_a, 32), 32), :]
        out_b[pl.ds(32 * n, 32), :] = stage[pl.ds(pl.multiple_of(32 * to_b, 32), 32), :]


def assemble_kernel(got_a, got_b, states, corrected, advanced, residual):
    interval = lax.axis_index("z") * PLACES + lax.axis_index("place")
    odd = lax.rem(lax.axis_index("space"), 2)
    blocks = []
    for tracer in range(2):
        for n in range(3):
            halves = []
            for j in range(2):
                rows = pl.ds(32 * n + j, 16, stride=2)
                halves.append(jnp.where(odd == tracer, got_a[rows, :], got_b[rows, :]))
            blocks.append(jnp.concatenate(halves, 1))
    moved = permuted(jnp.concatenate(blocks, 0), split_matrix(True))
    for tracer in range(2):
        c, a, r = (moved[16 * (3 * tracer + n) : 16 * (3 * tracer + n) + 16] for n in range(3))
        corrected[0, tracer] = jnp.where(interval == 0, states[0, tracer], c)
        advanced[0, tracer] = a
        residual[0, tracer] = jnp.where(interval <= 1, 0.0, r)


def call(kernel, out_shapes, scratch, operands, flops):
    shapes = [jax.ShapeDtypeStruct(shape, F32) for shape in out_shapes]
    moved = 4 * sum(int(np.prod(shape)) for shape in list(out_shapes) + [x.shape for x in operands])
    return pl.pallas_call(
        kernel,
        out_shape=shapes,
        in_specs=[VMEM] * len(operands),
        out_specs=[VMEM] * len(shapes),
        scratch_shapes=scratch,
        compiler_params=pltpu.CompilerParams(vmem_limit_bytes=24 * 2**20),
        cost_estimate=pl.CostEstimate(flops=flops, bytes_accessed=moved, transcendentals=0),
    )(*operands)


def on_device(states, vel_x, vel_y, diffus):
    field = (TILES, 8, 128)
    (pieces,) = call(prepare_kernel, [(PARTS, 32, 128)], [], [states], 10**6)
    whole = lax.all_to_all(pieces, "space", 0, 0, tiled=True).reshape(128, 128)
    following = lax.ppermute(whole, ("z", "place"), [(i + 1, i) for i in range(INTERVALS - 1)])
    levels, carried, forcing = call(
        own_kernel,
        [(3, *field), field, (PLANES, *field)],
        [pltpu.VMEM((128, 128), F32), coef_scratch(1), coef_scratch(1), coef_scratch(2), coef_scratch(2)],
        [whole, vel_x, vel_y, diffus],
        10**7,
    )
    forcings = lax.all_to_all(forcing, "z", 0, 0, tiled=True)
    (sums,) = call(
        planes_kernel,
        [(PLACES, *field)],
        [pltpu.VMEM(field, F32), coef_scratch(1), coef_scratch(2), coef_scratch(3)],
        [forcings, levels],
        10**8,
    )
    sums = lax.all_to_all(sums, "place", 0, 0, tiled=True)
    to_a, to_b = call(
        finish_kernel,
        [(96, 128), (96, 128)],
        [pltpu.VMEM(field, F32), pltpu.VMEM(field, F32), pltpu.VMEM((128, 128), F32)]
        + [coef_scratch(1), coef_scratch(2), coef_scratch(1), coef_scratch(2), coef_scratch(3)],
        [sums, following, carried, levels],
        10**7,
    )
    axes = ("z", "place", "space")

    def route(place_of):
        return [
            (q * PARTS + part, (q + 2) % INTERVALS * PARTS + place_of(part))
            for q in range(INTERVALS)
            for part in range(PARTS)
        ]

    got_a = lax.ppermute(to_a, axes, route(lambda part: 2 * (part % 2) + part // 2))
    got_b = lax.ppermute(to_b, axes, route(lambda part: 2 * (part % 2) + 1 - part // 2))
    return tuple(call(assemble_kernel, [(1, 2, 16, COLS)] * 3, [], [got_a, got_b, states], 10**7))


def solution(mesh):
    grid = Mesh(mesh.devices.reshape(PLANES, PLACES, PARTS), ("z", "place", "space"))
    split = P(("z", "place"), None, "space", None)
    return jax.shard_map(
        on_device,
        mesh=grid,
        in_specs=(split, P(), P(), P()),
        out_specs=(split, split, split),
        check_vma=False,
    )
```

```python
import functools

import jax
import jax.numpy as jnp
import numpy as np
from jax import lax
from jax.experimental import pallas as pl
from jax.experimental.pallas import tpu as pltpu
from jax.sharding import Mesh
from jax.sharding import PartitionSpec as P

STEPS = 16
ROWS, COLS = 64, 256
PLANES, PLACES, PARTS = 8, 8, 4
INTERVALS = PLANES * PLACES
TILES = 16
VMEM = pl.BlockSpec(memory_space=pltpu.VMEM)
F32, BF16 = jnp.float32, jnp.bfloat16


def diamond(radius):
    reach = range(-radius, radius + 1)
    return [(dr, dc) for dr in reach for dc in reach if abs(dr) + abs(dc) <= radius]


class Shifted:
    def __init__(self, tiles):
        self.tiles, self.made = tiles, {}

    def at(self, i, column):
        lanes, j = divmod(column, 2)
        key = (i, j, lanes)
        if key not in self.made:
            if not 0 <= i < 8:
                self.made[key] = pltpu.roll(self.at(i % 8, column), 1 if i < 0 else 7, 0)
            elif lanes:
                self.made[key] = pltpu.roll(self.tiles[2 * i + j], (-lanes) % 128, 1)
            else:
                self.made[key] = self.tiles[2 * i + j]
        return self.made[key]


def apply(tiles, coef, radius):
    moved, points, result = Shifted(tiles), diamond(radius), []
    for i in range(8):
        for j in range(2):
            order = sorted(range(len(points)), key=lambda n: (abs((j + points[n][1]) // 2), points[n][1], points[n][0]))
            total = None
            for n in order:
                term = coef[n, 2 * i + j] * moved.at(i + points[n][0], j + points[n][1])
                total = term if total is None else total + term
            result.append(total)
    return tuple(result)


def five_point(levels, tracer, factor, out):
    lane = lax.broadcasted_iota(jnp.int32, (8, 128), 1)
    sublane = lax.broadcasted_iota(jnp.int32, (8, 128), 0)
    scale = jnp.where(tracer == 0, 1.0, 0.5).astype(F32)
    offsets = diamond(1)
    for i in range(8):
        for j in range(2):
            k = 2 * i + j
            courant_x, courant_y = 0.01 * levels[0, k], 0.01 * levels[1, k]
            spread = scale * (0.005 * levels[2, k])
            above = factor * (spread + jnp.maximum(courant_x, 0.0))
            below = factor * (spread - jnp.minimum(courant_x, 0.0))
            left = factor * (spread + jnp.maximum(courant_y, 0.0))
            right = factor * (spread - jnp.minimum(courant_y, 0.0))
            middle = 1.0 - factor * (4.0 * spread + jnp.abs(courant_x) + jnp.abs(courant_y))
            if i == 0:
                above = jnp.where(sublane == 0, 0.0, above)
            if i == 7:
                below = jnp.where(sublane == 7, 0.0, below)
            if j == 0:
                left = jnp.where(lane == 0, 0.0, left)
            if j == 1:
                right = jnp.where(lane == 127, 0.0, right)
            for offset, value in (((0, 0), middle), ((-1, 0), above), ((1, 0), below), ((0, -1), left), ((0, 1), right)):
                out[offsets.index(offset), k] = value


def compose(one, source, radius, out):
    near, old = diamond(1), diamond(radius)
    for n, (row, column) in enumerate(diamond(radius + 1)):
        totals = [None] * TILES
        for m, (dr, dc) in enumerate(near):
            if (row - dr, column - dc) not in old:
                continue
            at = old.index((row - dr, column - dc))
            moved = Shifted([source[at, k] for k in range(TILES)])
            for k in range(TILES):
                term = one[m, k] * moved.at(k // 2 + dr, k % 2 + dc)
                totals[k] = term if totals[k] is None else totals[k] + term
        for k in range(TILES):
            out[n, k] = totals[k]


def coef_scratch(radius):
    return pltpu.VMEM((len(diamond(radius)), TILES, 8, 128), F32)


def load_flat(ref, start=0):
    return tuple(ref[pl.ds(start + 2 * i + j, 8, stride=16), :] for i in range(8) for j in range(2))


def store_flat(ref, tiles):
    for i in range(8):
        for j in range(2):
            ref[pl.ds(2 * i + j, 8, stride=16), :] = tiles[2 * i + j]


def load_tiles(ref, *at):
    return tuple(ref[(*at, k)] for k in range(TILES))


def store_tiles(ref, tiles, *at):
    for k in range(TILES):
        ref[(*at, k)] = tiles[k]


def added(a, b):
    return tuple(x + y for x, y in zip(a, b, strict=True))


def split_matrix(back):
    row = lax.broadcasted_iota(jnp.int32, (COLS, COLS), 0)
    column = lax.broadcasted_iota(jnp.int32, (COLS, COLS), 1)
    if back:
        row, column = column, row
    return jnp.where(row == 2 * (column % 128) + column // 128, 1.0, 0.0).astype(BF16)


def permuted(x, matrix):
    high = x.astype(BF16)
    rest = x - high.astype(F32)
    middle = rest.astype(BF16)
    low = (rest - middle.astype(F32)).astype(BF16)
    dot = functools.partial(jnp.dot, preferred_element_type=F32)
    return (dot(high, matrix) + dot(middle, matrix)) + dot(low, matrix)


def prepare_kernel(states, out):
    both = jnp.concatenate([states[0, 0], states[0, 1]], 0)
    moved = permuted(both, split_matrix(False))
    for part in range(PARTS):
        rows = moved[16 * (part % 2) : 16 * (part % 2) + 16]
        for j in range(2):
            out[part, pl.ds(j, 16, stride=2), :] = rows[:, 128 * j : 128 * j + 128]


def read_levels(tables, levels, stage):
    matrix = split_matrix(False)
    for n, table in enumerate(range(3)):
        moved = jnp.dot(tables[table].astype(F32).astype(BF16), matrix, preferred_element_type=F32)
        for j in range(2):
            stage[pl.ds(j, ROWS, stride=2), :] = moved[:, 128 * j : 128 * j + 128]
        store_tiles(levels, load_flat(stage), n)


def steps_of(levels, factor, out):
    five_point(levels, lax.rem(lax.axis_index("space"), 2), factor, out[0])
    for n in range(len(out) - 1):
        compose(out[0], out[n], n + 1, out[n + 1])


def fine_interval(fields, fine2):
    return lax.fori_loop(0, STEPS // 2, lambda _, now: tuple(apply(field, fine2, 2) for field in now), fields)


def coarse_steps(tiles, count, coarse, planes):
    turns = jnp.where(lax.axis_index("z") >= planes, count // 3, 0)
    tiles = lax.fori_loop(0, turns, lambda _, now: apply(now, coarse[2], 3), tiles)
    return apply(tiles, coarse[count % 3 - 1], count % 3) if count % 3 else tiles


def coarse_interval(tiles, coarse):
    return apply(apply(apply(tiles, coarse[2], 3), coarse[2], 3), coarse[1], 2)


def where_me():
    return lax.axis_index("z") * PLACES + lax.axis_index("place")


def force(tiles, first, fine2, coarse):
    def body(_, fields):
        ahead, image = fields
        return apply(apply(ahead, fine2, 2), fine2, 2), apply(image, coarse[1], 2)

    ahead, image = lax.fori_loop(0, STEPS // 4, body, (tiles, tiles))
    return ahead, tuple(jnp.where(first, a, a - i) for a, i in zip(ahead, image, strict=True))


def own_kernel(whole, tables, fine2, coarse1, coarse2, coarse3, carried, forcing, stage, levels, fine1):
    read_levels(tables, levels, stage)
    steps_of(levels, 1.0, (fine1, fine2))
    steps_of(levels, 2.0, (coarse1, coarse2, coarse3))
    ahead, forced = force(load_flat(whole), where_me() == 0, fine2, (coarse1, coarse2))
    store_tiles(carried, ahead)
    store_tiles(forcing, forced)


def pair_kernel(behind, forcing, fine2, coarse1, coarse2, coarse3, before, pair):
    coarse = (coarse1, coarse2, coarse3)
    _, forced = force(load_flat(behind), where_me() == PLACES, fine2, coarse)
    store_tiles(before, forced)
    store_tiles(pair, added(coarse_steps(forced, 64, coarse, 1), load_tiles(forcing)))


def far_kernel(sixth, coarse1, coarse2, coarse3, out):
    store_tiles(out, coarse_steps(load_tiles(sixth), 128, (coarse1, coarse2, coarse3), 6))


def near_kernel(far, fourth, coarse1, coarse2, coarse3, out):
    total = added(load_tiles(far), load_tiles(fourth))
    store_tiles(out, coarse_steps(total, 128, (coarse1, coarse2, coarse3), 4))


def planes_kernel(near, second, before, forcing, whole, last, ahead, coarse1, coarse2, coarse3, out, gap, past, earlier):
    place, coarse = lax.axis_index("place"), (coarse1, coarse2, coarse3)
    total = added(load_tiles(near), load_tiles(second))
    store_tiles(earlier, total)
    total = added(coarse_steps(total, 64, coarse, 2), load_tiles(before))
    store_tiles(past, total)
    total = added(coarse_steps(total, 64, coarse, 1), load_tiles(forcing))
    store_tiles(gap, tuple(a - b for a, b in zip(load_tiles(ahead), load_flat(last), strict=True)))
    start = load_flat(whole)
    for target in range(PLACES):
        for k in range(TILES):
            value = jnp.where(place <= target - 2, total[k], past[k])
            if target == 0:
                value = jnp.where(place == PLACES - 1, earlier[k], value)
            if target == 1:
                value = jnp.where(where_me() == 0, start[k], value)
            out[target, k] = value


def finish_kernel(sums, gap, carried, fine2, coarse2, coarse3, give, keep, corrected, stage):
    place, part, me = lax.axis_index("place"), lax.axis_index("space"), where_me()
    coarse = (None, coarse2, coarse3)

    def neighbour(k, tiles):
        return added(coarse_interval(tiles, coarse), load_tiles(sums, lax.rem(place + 7 + k, PLACES)))

    total = lax.fori_loop(1, PLACES, neighbour, load_tiles(sums, lax.rem(place + 7, PLACES)))
    total = tuple(jnp.where(me == 1, sums[0, k], t) for k, t in enumerate(total))
    (total,) = fine_interval((total,), fine2)
    store_tiles(corrected, total)
    advanced, residual = fine_interval((total, load_tiles(gap)), fine2)
    advanced = tuple(jnp.where(me == 0, c, a) for c, a in zip(load_tiles(carried), advanced, strict=True))
    other = part + 1 - 2 * lax.rem(part, 2)
    for n, tiles in enumerate((load_tiles(corrected), advanced, residual)):
        store_flat(stage, tiles)
        give[pl.ds(32 * n, 32), :] = stage[pl.ds(pl.multiple_of(32 * other, 32), 32), :]
        keep[pl.ds(32 * n, 32), :] = stage[pl.ds(pl.multiple_of(32 * part, 32), 32), :]


def assemble_kernel(got, kept, states, corrected, advanced, residual):
    interval, own = where_me(), lax.rem(lax.axis_index("space"), 2)
    blocks = []
    for tracer in range(2):
        for n in range(3):
            halves = []
            for j in range(2):
                rows = pl.ds(32 * n + j, 16, stride=2)
                halves.append(jnp.where(own == tracer, kept[rows, :], got[rows, :]))
            blocks.append(jnp.concatenate(halves, 1))
    moved = permuted(jnp.concatenate(blocks, 0), split_matrix(True))
    for tracer in range(2):
        c, a, r = (moved[16 * (3 * tracer + n) : 16 * (3 * tracer + n) + 16] for n in range(3))
        corrected[0, tracer] = jnp.where(interval == 0, states[0, tracer], c)
        advanced[0, tracer] = a
        residual[0, tracer] = jnp.where(interval <= 1, 0.0, r)


def call(kernel, out_shapes, scratch, operands, flops):
    shapes = [jax.ShapeDtypeStruct(shape, F32) for shape in out_shapes]
    moved = 4 * sum(int(np.prod(x.shape)) for x in [*shapes, *operands])
    return pl.pallas_call(
        kernel,
        out_shape=shapes,
        in_specs=[VMEM] * len(operands),
        out_specs=[VMEM] * len(shapes),
        scratch_shapes=scratch,
        compiler_params=pltpu.CompilerParams(vmem_limit_bytes=24 * 2**20),
        cost_estimate=pl.CostEstimate(flops=flops, bytes_accessed=moved, transcendentals=0),
    )(*operands)


def on_device(states, vel_x, vel_y, diffus):
    field, axes = (TILES, 8, 128), ("z", "place")

    def onward(value, steps):
        return lax.ppermute(value, axes, [(i, i + steps) for i in range(INTERVALS - steps)])

    (pieces,) = call(prepare_kernel, [(PARTS, 32, 128)], [], [states], 10**6)
    whole = lax.all_to_all(pieces, "space", 0, 0, tiled=True).reshape(128, 128)
    behind = onward(whole, PLACES)
    stage = pltpu.VMEM((128, 128), F32)
    fine2, coarse1, coarse2, coarse3, carried, forcing = call(
        own_kernel,
        [(len(diamond(radius)), *field) for radius in (2, 1, 2, 3)] + [field, field],
        [stage, pltpu.VMEM((3, *field), F32), coef_scratch(1)],
        [whole, jnp.stack([vel_x, vel_y, diffus])],
        10**7,
    )
    coarse = [coarse1, coarse2, coarse3]
    before, pair = call(pair_kernel, [field, field], [], [behind, forcing, fine2, *coarse], 3 * 10**7)
    sixth, fourth, second = (onward(pair, planes * PLACES) for planes in (6, 4, 2))
    last, ahead = onward(whole, 1), onward(carried, 2)
    (far,) = call(far_kernel, [field], [], [sixth, *coarse], 5 * 10**7)
    (near,) = call(near_kernel, [field], [], [far, fourth, *coarse], 5 * 10**7)
    sums, gap = call(
        planes_kernel,
        [(PLACES, *field), field],
        [pltpu.VMEM(field, F32), pltpu.VMEM(field, F32)],
        [near, second, before, forcing, whole, last, ahead, *coarse],
        5 * 10**7,
    )
    sums = lax.all_to_all(sums, "place", 0, 0, tiled=True)
    give, keep = call(
        finish_kernel,
        [(96, 128), (96, 128)],
        [pltpu.VMEM(field, F32), stage],
        [sums, gap, carried, fine2, coarse2, coarse3],
        3 * 10**7,
    )
    got = lax.ppermute(give, "space", [(part, part ^ 1) for part in range(PARTS)])
    return tuple(call(assemble_kernel, [(1, 2, 16, COLS)] * 3, [], [got, keep, states], 10**7))


def solution(mesh):
    grid = Mesh(mesh.devices.reshape(PLANES, PLACES, PARTS), ("z", "place", "space"))
    split = P(("z", "place"), None, "space", None)
    return jax.shard_map(
        on_device,
        mesh=grid,
        in_specs=(split, P(), P(), P()),
        out_specs=(split, split, split),
        check_vma=False,
    )
```

```python
import functools

import jax
import jax.numpy as jnp
import numpy as np
from jax import lax
from jax.experimental import pallas as pl
from jax.experimental.pallas import tpu as pltpu
from jax.sharding import Mesh
from jax.sharding import PartitionSpec as P

STEPS = 16
ROWS, COLS = 64, 256
PLANES, PLACES, PARTS = 8, 8, 4
INTERVALS = PLANES * PLACES
TILES = 16
VMEM = pl.BlockSpec(memory_space=pltpu.VMEM)
F32, BF16 = jnp.float32, jnp.bfloat16


def diamond(radius):
    reach = range(-radius, radius + 1)
    return [(dr, dc) for dr in reach for dc in reach if abs(dr) + abs(dc) <= radius]


class Shifted:
    def __init__(self, tiles):
        self.tiles, self.made = tiles, {}

    def at(self, i, column):
        lanes, j = divmod(column, 2)
        key = (i, j, lanes)
        if key not in self.made:
            if not 0 <= i < 8:
                self.made[key] = pltpu.roll(self.at(i % 8, column), 1 if i < 0 else 7, 0)
            elif lanes:
                self.made[key] = pltpu.roll(self.tiles[2 * i + j], (-lanes) % 128, 1)
            else:
                self.made[key] = self.tiles[2 * i + j]
        return self.made[key]


def apply(tiles, coef, radius):
    moved, points, result = Shifted(tiles), diamond(radius), []
    for i in range(8):
        for j in range(2):
            order = sorted(range(len(points)), key=lambda n: (abs((j + points[n][1]) // 2), points[n][1], points[n][0]))
            total = None
            for n in order:
                term = coef[n, 2 * i + j] * moved.at(i + points[n][0], j + points[n][1])
                total = term if total is None else total + term
            result.append(total)
    return tuple(result)


def five_point(levels, tracer, factor, out):
    lane = lax.broadcasted_iota(jnp.int32, (8, 128), 1)
    sublane = lax.broadcasted_iota(jnp.int32, (8, 128), 0)
    scale = jnp.where(tracer == 0, 1.0, 0.5).astype(F32)
    offsets = diamond(1)
    for i in range(8):
        for j in range(2):
            k = 2 * i + j
            courant_x, courant_y = 0.01 * levels[0, k], 0.01 * levels[1, k]
            spread = scale * (0.005 * levels[2, k])
            above = factor * (spread + jnp.maximum(courant_x, 0.0))
            below = factor * (spread - jnp.minimum(courant_x, 0.0))
            left = factor * (spread + jnp.maximum(courant_y, 0.0))
            right = factor * (spread - jnp.minimum(courant_y, 0.0))
            middle = 1.0 - factor * (4.0 * spread + jnp.abs(courant_x) + jnp.abs(courant_y))
            if i == 0:
                above = jnp.where(sublane == 0, 0.0, above)
            if i == 7:
                below = jnp.where(sublane == 7, 0.0, below)
            if j == 0:
                left = jnp.where(lane == 0, 0.0, left)
            if j == 1:
                right = jnp.where(lane == 127, 0.0, right)
            for offset, value in (((0, 0), middle), ((-1, 0), above), ((1, 0), below), ((0, -1), left), ((0, 1), right)):
                out[offsets.index(offset), k] = value


def compose(one, source, radius, out):
    near, old = diamond(1), diamond(radius)
    for n, (row, column) in enumerate(diamond(radius + 1)):
        totals = [None] * TILES
        for m, (dr, dc) in enumerate(near):
            if (row - dr, column - dc) not in old:
                continue
            at = old.index((row - dr, column - dc))
            moved = Shifted([source[at, k] for k in range(TILES)])
            for k in range(TILES):
                term = one[m, k] * moved.at(k // 2 + dr, k % 2 + dc)
                totals[k] = term if totals[k] is None else totals[k] + term
        for k in range(TILES):
            out[n, k] = totals[k]


def coef_scratch(radius):
    return pltpu.VMEM((len(diamond(radius)), TILES, 8, 128), F32)


def load_flat(ref, start=0):
    return tuple(ref[pl.ds(start + 2 * i + j, 8, stride=16), :] for i in range(8) for j in range(2))


def store_flat(ref, tiles):
    for i in range(8):
        for j in range(2):
            ref[pl.ds(2 * i + j, 8, stride=16), :] = tiles[2 * i + j]


def load_tiles(ref, *at):
    return tuple(ref[(*at, k)] for k in range(TILES))


def store_tiles(ref, tiles, *at):
    for k in range(TILES):
        ref[(*at, k)] = tiles[k]


def added(a, b):
    return tuple(x + y for x, y in zip(a, b, strict=True))


def split_matrix(back):
    row = lax.broadcasted_iota(jnp.int32, (COLS, COLS), 0)
    column = lax.broadcasted_iota(jnp.int32, (COLS, COLS), 1)
    if back:
        row, column = column, row
    return jnp.where(row == 2 * (column % 128) + column // 128, 1.0, 0.0).astype(BF16)


def permuted(x, matrix):
    high = x.astype(BF16)
    rest = x - high.astype(F32)
    middle = rest.astype(BF16)
    low = (rest - middle.astype(F32)).astype(BF16)
    dot = functools.partial(jnp.dot, preferred_element_type=F32)
    return (dot(high, matrix) + dot(middle, matrix)) + dot(low, matrix)


def prepare_kernel(states, out):
    both = jnp.concatenate([states[0, 0], states[0, 1]], 0)
    moved = permuted(both, split_matrix(False))
    for part in range(PARTS):
        rows = moved[16 * (part % 2) : 16 * (part % 2) + 16]
        for j in range(2):
            out[part, pl.ds(j, 16, stride=2), :] = rows[:, 128 * j : 128 * j + 128]


def read_levels(tables, levels, stage):
    matrix = split_matrix(False)
    for n, table in enumerate(range(3)):
        moved = jnp.dot(tables[table].astype(F32).astype(BF16), matrix, preferred_element_type=F32)
        for j in range(2):
            stage[pl.ds(j, ROWS, stride=2), :] = moved[:, 128 * j : 128 * j + 128]
        store_tiles(levels, load_flat(stage), n)


def steps_of(levels, factor, out):
    five_point(levels, lax.rem(lax.axis_index("space"), 2), factor, out[0])
    for n in range(len(out) - 1):
        compose(out[0], out[n], n + 1, out[n + 1])


def fine_interval(fields, fine2):
    return lax.fori_loop(0, STEPS // 2, lambda _, now: tuple(apply(field, fine2, 2) for field in now), fields)


def coarse_steps(tiles, count, coarse, planes):
    turns = jnp.where(lax.axis_index("z") >= planes, count // 9, 0)

    def body(_, now):
        for _ in range(3):
            now = apply(now, coarse[2], 3)
        return now

    tiles = lax.fori_loop(0, turns, body, tiles)
    count -= count // 9 * 9
    return apply(tiles, coarse[count % 3 - 1], count % 3) if count % 3 else tiles


def coarse_interval(tiles, coarse):
    return apply(apply(apply(tiles, coarse[2], 3), coarse[2], 3), coarse[1], 2)


def where_me():
    return lax.axis_index("z") * PLACES + lax.axis_index("place")


def force(tiles, first, fine2, coarse):
    def body(_, fields):
        ahead, image = fields
        return apply(apply(ahead, fine2, 2), fine2, 2), apply(image, coarse[1], 2)

    ahead, image = lax.fori_loop(0, STEPS // 4, body, (tiles, tiles))
    return ahead, tuple(jnp.where(first, a, a - i) for a, i in zip(ahead, image, strict=True))


def own_kernel(whole, tables, fine2, coarse1, coarse2, coarse3, carried, forcing, stage, levels, fine1):
    read_levels(tables, levels, stage)
    steps_of(levels, 1.0, (fine1, fine2))
    steps_of(levels, 2.0, (coarse1, coarse2, coarse3))
    ahead, forced = force(load_flat(whole), where_me() == 0, fine2, (coarse1, coarse2))
    store_tiles(carried, ahead)
    store_tiles(forcing, forced)


def pair_kernel(behind, forcing, fine2, coarse1, coarse2, coarse3, before, pair):
    coarse = (coarse1, coarse2, coarse3)
    _, forced = force(load_flat(behind), where_me() == PLACES, fine2, coarse)
    store_tiles(before, forced)
    store_tiles(pair, added(coarse_steps(forced, 64, coarse, 1), load_tiles(forcing)))


def far_kernel(sixth, coarse1, coarse2, coarse3, out):
    store_tiles(out, coarse_steps(load_tiles(sixth), 128, (coarse1, coarse2, coarse3), 6))


def near_kernel(far, fourth, coarse1, coarse2, coarse3, out):
    total = added(load_tiles(far), load_tiles(fourth))
    store_tiles(out, coarse_steps(total, 128, (coarse1, coarse2, coarse3), 4))


def planes_kernel(near, second, before, forcing, whole, last, ahead, coarse1, coarse2, coarse3, out, gap, past, earlier):
    place, coarse = lax.axis_index("place"), (coarse1, coarse2, coarse3)
    total = added(load_tiles(near), load_tiles(second))
    store_tiles(earlier, total)
    total = added(coarse_steps(total, 64, coarse, 2), load_tiles(before))
    store_tiles(past, total)
    total = added(coarse_steps(total, 64, coarse, 1), load_tiles(forcing))
    store_tiles(gap, tuple(a - b for a, b in zip(load_tiles(ahead), load_flat(last), strict=True)))
    start = load_flat(whole)
    for target in range(PLACES):
        for k in range(TILES):
            value = jnp.where(place <= target - 2, total[k], past[k])
            if target == 0:
                value = jnp.where(place == PLACES - 1, earlier[k], value)
            if target == 1:
                value = jnp.where(where_me() == 0, start[k], value)
            out[target, k] = value


def finish_kernel(sums, gap, carried, fine2, coarse2, coarse3, give, keep, corrected, stage):
    place, part, me = lax.axis_index("place"), lax.axis_index("space"), where_me()
    coarse = (None, coarse2, coarse3)

    def neighbour(k, tiles):
        return added(coarse_interval(tiles, coarse), load_tiles(sums, lax.rem(place + 7 + k, PLACES)))

    total = lax.fori_loop(1, PLACES, neighbour, load_tiles(sums, lax.rem(place + 7, PLACES)))
    total = tuple(jnp.where(me == 1, sums[0, k], t) for k, t in enumerate(total))
    (total,) = fine_interval((total,), fine2)
    store_tiles(corrected, total)
    advanced, residual = fine_interval((total, load_tiles(gap)), fine2)
    advanced = tuple(jnp.where(me == 0, c, a) for c, a in zip(load_tiles(carried), advanced, strict=True))
    other = part + 1 - 2 * lax.rem(part, 2)
    for n, tiles in enumerate((load_tiles(corrected), advanced, residual)):
        store_flat(stage, tiles)
        give[pl.ds(32 * n, 32), :] = stage[pl.ds(pl.multiple_of(32 * other, 32), 32), :]
        keep[pl.ds(32 * n, 32), :] = stage[pl.ds(pl.multiple_of(32 * part, 32), 32), :]


def assemble_kernel(got, kept, states, corrected, advanced, residual):
    interval, own = where_me(), lax.rem(lax.axis_index("space"), 2)
    blocks = []
    for tracer in range(2):
        for n in range(3):
            halves = []
            for j in range(2):
                rows = pl.ds(32 * n + j, 16, stride=2)
                halves.append(jnp.where(own == tracer, kept[rows, :], got[rows, :]))
            blocks.append(jnp.concatenate(halves, 1))
    moved = permuted(jnp.concatenate(blocks, 0), split_matrix(True))
    for tracer in range(2):
        c, a, r = (moved[16 * (3 * tracer + n) : 16 * (3 * tracer + n) + 16] for n in range(3))
        corrected[0, tracer] = jnp.where(interval == 0, states[0, tracer], c)
        advanced[0, tracer] = a
        residual[0, tracer] = jnp.where(interval <= 1, 0.0, r)


def call(kernel, out_shapes, scratch, operands, flops):
    shapes = [jax.ShapeDtypeStruct(shape, F32) for shape in out_shapes]
    moved = 4 * sum(int(np.prod(x.shape)) for x in [*shapes, *operands])
    return pl.pallas_call(
        kernel,
        out_shape=shapes,
        in_specs=[VMEM] * len(operands),
        out_specs=[VMEM] * len(shapes),
        scratch_shapes=scratch,
        compiler_params=pltpu.CompilerParams(vmem_limit_bytes=24 * 2**20),
        cost_estimate=pl.CostEstimate(flops=flops, bytes_accessed=moved, transcendentals=0),
    )(*operands)


def on_device(states, vel_x, vel_y, diffus):
    field, axes = (TILES, 8, 128), ("z", "place")

    def onward(value, steps):
        return lax.ppermute(value, axes, [(i, i + steps) for i in range(INTERVALS - steps)])

    (pieces,) = call(prepare_kernel, [(PARTS, 32, 128)], [], [states], 10**6)
    whole = lax.all_to_all(pieces, "space", 0, 0, tiled=True).reshape(128, 128)
    behind = onward(whole, PLACES)
    stage = pltpu.VMEM((128, 128), F32)
    fine2, coarse1, coarse2, coarse3, carried, forcing = call(
        own_kernel,
        [(len(diamond(radius)), *field) for radius in (2, 1, 2, 3)] + [field, field],
        [stage, pltpu.VMEM((3, *field), F32), coef_scratch(1)],
        [whole, jnp.stack([vel_x, vel_y, diffus])],
        10**7,
    )
    coarse = [coarse1, coarse2, coarse3]
    before, pair = call(pair_kernel, [field, field], [], [behind, forcing, fine2, *coarse], 3 * 10**7)
    sixth, fourth, second = (onward(pair, planes * PLACES) for planes in (6, 4, 2))
    last, ahead = onward(whole, 1), onward(carried, 2)
    (far,) = call(far_kernel, [field], [], [sixth, *coarse], 5 * 10**7)
    (near,) = call(near_kernel, [field], [], [far, fourth, *coarse], 5 * 10**7)
    sums, gap = call(
        planes_kernel,
        [(PLACES, *field), field],
        [pltpu.VMEM(field, F32), pltpu.VMEM(field, F32)],
        [near, second, before, forcing, whole, last, ahead, *coarse],
        5 * 10**7,
    )
    sums = lax.all_to_all(sums, "place", 0, 0, tiled=True)
    give, keep = call(
        finish_kernel,
        [(96, 128), (96, 128)],
        [pltpu.VMEM(field, F32), stage],
        [sums, gap, carried, fine2, coarse2, coarse3],
        3 * 10**7,
    )
    got = lax.ppermute(give, "space", [(part, part ^ 1) for part in range(PARTS)])
    return tuple(call(assemble_kernel, [(1, 2, 16, COLS)] * 3, [], [got, keep, states], 10**7))


def solution(mesh):
    grid = Mesh(mesh.devices.reshape(PLANES, PLACES, PARTS), ("z", "place", "space"))
    split = P(("z", "place"), None, "space", None)
    return jax.shard_map(
        on_device,
        mesh=grid,
        in_specs=(split, P(), P(), P()),
        out_specs=(split, split, split),
        check_vma=False,
    )
```

```python
import functools

import jax
import jax.numpy as jnp
import numpy as np
from jax import lax
from jax.experimental import pallas as pl
from jax.experimental.pallas import tpu as pltpu
from jax.sharding import Mesh
from jax.sharding import PartitionSpec as P

STEPS = 16
ROWS, COLS = 64, 256
PLANES, PLACES, PARTS = 8, 8, 4
INTERVALS = PLANES * PLACES
TILES = 16
VMEM = pl.BlockSpec(memory_space=pltpu.VMEM)
F32, BF16 = jnp.float32, jnp.bfloat16


def diamond(radius):
    reach = range(-radius, radius + 1)
    return [(dr, dc) for dr in reach for dc in reach if abs(dr) + abs(dc) <= radius]


class Shifted:
    def __init__(self, tiles):
        self.tiles, self.made = tiles, {}

    def at(self, i, column):
        lanes, j = divmod(column, 2)
        key = (i, j, lanes)
        if key not in self.made:
            if not 0 <= i < 8:
                self.made[key] = pltpu.roll(self.at(i % 8, column), 1 if i < 0 else 7, 0)
            elif lanes:
                self.made[key] = pltpu.roll(self.tiles[2 * i + j], (-lanes) % 128, 1)
            else:
                self.made[key] = self.tiles[2 * i + j]
        return self.made[key]


def apply(tiles, coef, radius):
    moved, points, result = Shifted(tiles), diamond(radius), []
    for i in range(8):
        for j in range(2):
            order = sorted(range(len(points)), key=lambda n: (abs((j + points[n][1]) // 2), points[n][1], points[n][0]))
            total = None
            for n in order:
                term = coef[n, 2 * i + j] * moved.at(i + points[n][0], j + points[n][1])
                total = term if total is None else total + term
            result.append(total)
    return tuple(result)


def five_point(levels, tracer, factor, out):
    lane = lax.broadcasted_iota(jnp.int32, (8, 128), 1)
    sublane = lax.broadcasted_iota(jnp.int32, (8, 128), 0)
    scale = jnp.where(tracer == 0, 1.0, 0.5).astype(F32)
    offsets = diamond(1)
    for i in range(8):
        for j in range(2):
            k = 2 * i + j
            courant_x, courant_y = 0.01 * levels[0, k], 0.01 * levels[1, k]
            spread = scale * (0.005 * levels[2, k])
            above = factor * (spread + jnp.maximum(courant_x, 0.0))
            below = factor * (spread - jnp.minimum(courant_x, 0.0))
            left = factor * (spread + jnp.maximum(courant_y, 0.0))
            right = factor * (spread - jnp.minimum(courant_y, 0.0))
            middle = 1.0 - factor * (4.0 * spread + jnp.abs(courant_x) + jnp.abs(courant_y))
            if i == 0:
                above = jnp.where(sublane == 0, 0.0, above)
            if i == 7:
                below = jnp.where(sublane == 7, 0.0, below)
            if j == 0:
                left = jnp.where(lane == 0, 0.0, left)
            if j == 1:
                right = jnp.where(lane == 127, 0.0, right)
            for offset, value in (((0, 0), middle), ((-1, 0), above), ((1, 0), below), ((0, -1), left), ((0, 1), right)):
                out[offsets.index(offset), k] = value


def compose(one, source, radius, out):
    near, old = diamond(1), diamond(radius)
    for n, (row, column) in enumerate(diamond(radius + 1)):
        totals = [None] * TILES
        for m, (dr, dc) in enumerate(near):
            if (row - dr, column - dc) not in old:
                continue
            at = old.index((row - dr, column - dc))
            moved = Shifted([source[at, k] for k in range(TILES)])
            for k in range(TILES):
                term = one[m, k] * moved.at(k // 2 + dr, k % 2 + dc)
                totals[k] = term if totals[k] is None else totals[k] + term
        for k in range(TILES):
            out[n, k] = totals[k]


def coef_scratch(radius):
    return pltpu.VMEM((len(diamond(radius)), TILES, 8, 128), F32)


def load_flat(ref, start=0):
    return tuple(ref[pl.ds(start + 2 * i + j, 8, stride=16), :] for i in range(8) for j in range(2))


def store_flat(ref, tiles):
    for i in range(8):
        for j in range(2):
            ref[pl.ds(2 * i + j, 8, stride=16), :] = tiles[2 * i + j]


def load_tiles(ref, *at):
    return tuple(ref[(*at, k)] for k in range(TILES))


def store_tiles(ref, tiles, *at):
    for k in range(TILES):
        ref[(*at, k)] = tiles[k]


def added(a, b):
    return tuple(x + y for x, y in zip(a, b, strict=True))


def split_matrix(back):
    row = lax.broadcasted_iota(jnp.int32, (COLS, COLS), 0)
    column = lax.broadcasted_iota(jnp.int32, (COLS, COLS), 1)
    if back:
        row, column = column, row
    return jnp.where(row == 2 * (column % 128) + column // 128, 1.0, 0.0).astype(BF16)


def permuted(x, matrix):
    high = x.astype(BF16)
    rest = x - high.astype(F32)
    middle = rest.astype(BF16)
    low = (rest - middle.astype(F32)).astype(BF16)
    dot = functools.partial(jnp.dot, preferred_element_type=F32)
    return (dot(high, matrix) + dot(middle, matrix)) + dot(low, matrix)


def prepare_kernel(states, out):
    both = jnp.concatenate([states[0, 0], states[0, 1]], 0)
    moved = permuted(both, split_matrix(False))
    for part in range(PARTS):
        rows = moved[16 * (part % 2) : 16 * (part % 2) + 16]
        for j in range(2):
            out[part, pl.ds(j, 16, stride=2), :] = rows[:, 128 * j : 128 * j + 128]


def read_levels(tables, levels, stage):
    matrix = split_matrix(False)
    for n, table in enumerate(range(3)):
        moved = jnp.dot(tables[table].astype(F32).astype(BF16), matrix, preferred_element_type=F32)
        for j in range(2):
            stage[pl.ds(j, ROWS, stride=2), :] = moved[:, 128 * j : 128 * j + 128]
        store_tiles(levels, load_flat(stage), n)


def steps_of(levels, factor, out):
    five_point(levels, lax.rem(lax.axis_index("space"), 2), factor, out[0])
    for n in range(len(out) - 1):
        compose(out[0], out[n], n + 1, out[n + 1])


def fine_interval(fields, fine2):
    return lax.fori_loop(0, STEPS // 2, lambda _, now: tuple(apply(field, fine2, 2) for field in now), fields)


def coarse_steps(tiles, count, coarse, planes, end=PLANES):
    plane = lax.axis_index("z")
    turns = jnp.where((plane >= planes) & (plane < end), count // 9, 0)

    def body(_, now):
        for _ in range(3):
            now = apply(now, coarse[2], 3)
        return now

    tiles = lax.fori_loop(0, turns, body, tiles)
    count -= count // 9 * 9
    return apply(tiles, coarse[count % 3 - 1], count % 3) if count % 3 else tiles


def coarse_interval(tiles, coarse):
    return apply(apply(apply(tiles, coarse[2], 3), coarse[2], 3), coarse[1], 2)


def where_me():
    return lax.axis_index("z") * PLACES + lax.axis_index("place")


def force(tiles, first, fine2, coarse):
    def body(_, fields):
        ahead, image = fields
        return apply(apply(ahead, fine2, 2), fine2, 2), apply(image, coarse[1], 2)

    ahead, image = lax.fori_loop(0, STEPS // 4, body, (tiles, tiles))
    return ahead, tuple(jnp.where(first, a, a - i) for a, i in zip(ahead, image, strict=True))


def own_kernel(whole, tables, fine2, coarse1, coarse2, coarse3, carried, forcing, stage, levels, fine1):
    read_levels(tables, levels, stage)
    steps_of(levels, 1.0, (fine1, fine2))
    steps_of(levels, 2.0, (coarse1, coarse2, coarse3))
    ahead, forced = force(load_flat(whole), where_me() == 0, fine2, (coarse1, coarse2))
    store_tiles(carried, ahead)
    store_tiles(forcing, forced)


def pair_kernel(behind, forcing, fine2, coarse1, coarse2, coarse3, before, pair):
    coarse = (coarse1, coarse2, coarse3)
    _, forced = force(load_flat(behind), where_me() == PLACES, fine2, coarse)
    store_tiles(before, forced)
    store_tiles(pair, added(coarse_steps(forced, 64, coarse, 1, PLANES - 2), load_tiles(forcing)))


def far_kernel(sixth, coarse1, coarse2, coarse3, out):
    store_tiles(out, coarse_steps(load_tiles(sixth), 128, (coarse1, coarse2, coarse3), 6))


def near_kernel(far, fourth, coarse1, coarse2, coarse3, out):
    total = added(load_tiles(far), load_tiles(fourth))
    store_tiles(out, coarse_steps(total, 128, (coarse1, coarse2, coarse3), 4))


def planes_kernel(near, second, before, forcing, whole, last, ahead, coarse1, coarse2, coarse3, out, gap, past, earlier):
    place, coarse = lax.axis_index("place"), (coarse1, coarse2, coarse3)
    total = added(load_tiles(near), load_tiles(second))
    store_tiles(earlier, total)
    total = added(coarse_steps(total, 64, coarse, 2), load_tiles(before))
    store_tiles(past, total)
    total = added(coarse_steps(total, 64, coarse, 1), load_tiles(forcing))
    store_tiles(gap, tuple(a - b for a, b in zip(load_tiles(ahead), load_flat(last), strict=True)))
    start = load_flat(whole)
    for target in range(PLACES):
        for k in range(TILES):
            value = jnp.where(place <= target - 2, total[k], past[k])
            if target == 0:
                value = jnp.where(place == PLACES - 1, earlier[k], value)
            if target == 1:
                value = jnp.where(where_me() == 0, start[k], value)
            out[target, k] = value


def finish_kernel(sums, gap, carried, fine2, coarse2, coarse3, give, keep, corrected, stage):
    place, part, me = lax.axis_index("place"), lax.axis_index("space"), where_me()
    coarse = (None, coarse2, coarse3)

    def neighbour(k, tiles):
        return added(coarse_interval(tiles, coarse), load_tiles(sums, lax.rem(place + 7 + k, PLACES)))

    total = lax.fori_loop(1, PLACES, neighbour, load_tiles(sums, lax.rem(place + 7, PLACES)))
    total = tuple(jnp.where(me == 1, sums[0, k], t) for k, t in enumerate(total))
    (total,) = fine_interval((total,), fine2)
    store_tiles(corrected, total)
    advanced, residual = fine_interval((total, load_tiles(gap)), fine2)
    advanced = tuple(jnp.where(me == 0, c, a) for c, a in zip(load_tiles(carried), advanced, strict=True))
    other = part + 1 - 2 * lax.rem(part, 2)
    for n, tiles in enumerate((load_tiles(corrected), advanced, residual)):
        store_flat(stage, tiles)
        give[pl.ds(32 * n, 32), :] = stage[pl.ds(pl.multiple_of(32 * other, 32), 32), :]
        keep[pl.ds(32 * n, 32), :] = stage[pl.ds(pl.multiple_of(32 * part, 32), 32), :]


def assemble_kernel(got, kept, states, corrected, advanced, residual):
    interval, own = where_me(), lax.rem(lax.axis_index("space"), 2)
    blocks = []
    for tracer in range(2):
        for n in range(3):
            halves = []
            for j in range(2):
                rows = pl.ds(32 * n + j, 16, stride=2)
                halves.append(jnp.where(own == tracer, kept[rows, :], got[rows, :]))
            blocks.append(jnp.concatenate(halves, 1))
    moved = permuted(jnp.concatenate(blocks, 0), split_matrix(True))
    for tracer in range(2):
        c, a, r = (moved[16 * (3 * tracer + n) : 16 * (3 * tracer + n) + 16] for n in range(3))
        corrected[0, tracer] = jnp.where(interval == 0, states[0, tracer], c)
        advanced[0, tracer] = a
        residual[0, tracer] = jnp.where(interval <= 1, 0.0, r)


def call(kernel, out_shapes, scratch, operands, flops):
    shapes = [jax.ShapeDtypeStruct(shape, F32) for shape in out_shapes]
    moved = 4 * sum(int(np.prod(x.shape)) for x in [*shapes, *operands])
    return pl.pallas_call(
        kernel,
        out_shape=shapes,
        in_specs=[VMEM] * len(operands),
        out_specs=[VMEM] * len(shapes),
        scratch_shapes=scratch,
        compiler_params=pltpu.CompilerParams(vmem_limit_bytes=24 * 2**20),
        cost_estimate=pl.CostEstimate(flops=flops, bytes_accessed=moved, transcendentals=0),
    )(*operands)


def on_device(states, vel_x, vel_y, diffus):
    field, axes = (TILES, 8, 128), ("z", "place")

    def onward(value, steps):
        return lax.ppermute(value, axes, [(i, i + steps) for i in range(INTERVALS - steps)])

    (pieces,) = call(prepare_kernel, [(PARTS, 32, 128)], [], [states], 10**6)
    whole = lax.all_to_all(pieces, "space", 0, 0, tiled=True).reshape(128, 128)
    behind = onward(whole, PLACES)
    stage = pltpu.VMEM((128, 128), F32)
    fine2, coarse1, coarse2, coarse3, carried, forcing = call(
        own_kernel,
        [(len(diamond(radius)), *field) for radius in (2, 1, 2, 3)] + [field, field],
        [stage, pltpu.VMEM((3, *field), F32), coef_scratch(1)],
        [whole, jnp.stack([vel_x, vel_y, diffus])],
        10**7,
    )
    coarse = [coarse1, coarse2, coarse3]
    before, pair = call(pair_kernel, [field, field], [], [behind, forcing, fine2, *coarse], 3 * 10**7)
    sixth, fourth, second = (onward(pair, planes * PLACES) for planes in (6, 4, 2))
    last, ahead = onward(whole, 1), onward(carried, 2)
    (far,) = call(far_kernel, [field], [], [sixth, *coarse], 5 * 10**7)
    (near,) = call(near_kernel, [field], [], [far, fourth, *coarse], 5 * 10**7)
    sums, gap = call(
        planes_kernel,
        [(PLACES, *field), field],
        [pltpu.VMEM(field, F32), pltpu.VMEM(field, F32)],
        [near, second, before, forcing, whole, last, ahead, *coarse],
        5 * 10**7,
    )
    sums = lax.all_to_all(sums, "place", 0, 0, tiled=True)
    give, keep = call(
        finish_kernel,
        [(96, 128), (96, 128)],
        [pltpu.VMEM(field, F32), stage],
        [sums, gap, carried, fine2, coarse2, coarse3],
        3 * 10**7,
    )
    got = lax.ppermute(give, "space", [(part, part ^ 1) for part in range(PARTS)])
    return tuple(call(assemble_kernel, [(1, 2, 16, COLS)] * 3, [], [got, keep, states], 10**7))


def solution(mesh):
    grid = Mesh(mesh.devices.reshape(PLANES, PLACES, PARTS), ("z", "place", "space"))
    split = P(("z", "place"), None, "space", None)
    return jax.shard_map(
        on_device,
        mesh=grid,
        in_specs=(split, P(), P(), P()),
        out_specs=(split, split, split),
        check_vma=False,
    )
```

```python
import functools

import jax
import jax.numpy as jnp
import numpy as np
from jax import lax
from jax.experimental import pallas as pl
from jax.experimental.pallas import tpu as pltpu
from jax.sharding import Mesh
from jax.sharding import PartitionSpec as P

STEPS = 16
ROWS, COLS = 64, 256
PLANES, PLACES, PARTS = 8, 8, 4
INTERVALS = PLANES * PLACES
TILES = 16
VMEM = pl.BlockSpec(memory_space=pltpu.VMEM)
F32, BF16 = jnp.float32, jnp.bfloat16


def diamond(radius):
    reach = range(-radius, radius + 1)
    return [(dr, dc) for dr in reach for dc in reach if abs(dr) + abs(dc) <= radius]


class Shifted:
    def __init__(self, tiles):
        self.tiles, self.made = tiles, {}

    def at(self, i, column):
        lanes, j = divmod(column, 2)
        key = (i, j, lanes)
        if key not in self.made:
            if not 0 <= i < 8:
                self.made[key] = pltpu.roll(self.at(i % 8, column), 1 if i < 0 else 7, 0)
            elif lanes:
                self.made[key] = pltpu.roll(self.tiles[2 * i + j], (-lanes) % 128, 1)
            else:
                self.made[key] = self.tiles[2 * i + j]
        return self.made[key]


def apply(tiles, coef, radius):
    moved, points, result = Shifted(tiles), diamond(radius), []
    for i in range(8):
        for j in range(2):
            order = sorted(range(len(points)), key=lambda n: (abs((j + points[n][1]) // 2), points[n][1], points[n][0]))
            total = None
            for n in order:
                term = coef[n, 2 * i + j] * moved.at(i + points[n][0], j + points[n][1])
                total = term if total is None else total + term
            result.append(total)
    return tuple(result)


def five_point(levels, tracer, factor, out):
    lane = lax.broadcasted_iota(jnp.int32, (8, 128), 1)
    sublane = lax.broadcasted_iota(jnp.int32, (8, 128), 0)
    scale = jnp.where(tracer == 0, 1.0, 0.5).astype(F32)
    offsets = diamond(1)
    for i in range(8):
        for j in range(2):
            k = 2 * i + j
            courant_x, courant_y = 0.01 * levels[0, k], 0.01 * levels[1, k]
            spread = scale * (0.005 * levels[2, k])
            above = factor * (spread + jnp.maximum(courant_x, 0.0))
            below = factor * (spread - jnp.minimum(courant_x, 0.0))
            left = factor * (spread + jnp.maximum(courant_y, 0.0))
            right = factor * (spread - jnp.minimum(courant_y, 0.0))
            middle = 1.0 - factor * (4.0 * spread + jnp.abs(courant_x) + jnp.abs(courant_y))
            if i == 0:
                above = jnp.where(sublane == 0, 0.0, above)
            if i == 7:
                below = jnp.where(sublane == 7, 0.0, below)
            if j == 0:
                left = jnp.where(lane == 0, 0.0, left)
            if j == 1:
                right = jnp.where(lane == 127, 0.0, right)
            for offset, value in (((0, 0), middle), ((-1, 0), above), ((1, 0), below), ((0, -1), left), ((0, 1), right)):
                out[offsets.index(offset), k] = value


def compose(one, source, radius, out):
    near, old = diamond(1), diamond(radius)
    for n, (row, column) in enumerate(diamond(radius + 1)):
        totals = [None] * TILES
        for m, (dr, dc) in enumerate(near):
            if (row - dr, column - dc) not in old:
                continue
            at = old.index((row - dr, column - dc))
            moved = Shifted([source[at, k] for k in range(TILES)])
            for k in range(TILES):
                term = one[m, k] * moved.at(k // 2 + dr, k % 2 + dc)
                totals[k] = term if totals[k] is None else totals[k] + term
        for k in range(TILES):
            out[n, k] = totals[k]


def coef_scratch(radius):
    return pltpu.VMEM((len(diamond(radius)), TILES, 8, 128), F32)


def load_flat(ref, start=0):
    return tuple(ref[pl.ds(start + 2 * i + j, 8, stride=16), :] for i in range(8) for j in range(2))


def store_flat(ref, tiles):
    for i in range(8):
        for j in range(2):
            ref[pl.ds(2 * i + j, 8, stride=16), :] = tiles[2 * i + j]


def load_tiles(ref, *at):
    return tuple(ref[(*at, k)] for k in range(TILES))


def store_tiles(ref, tiles, *at):
    for k in range(TILES):
        ref[(*at, k)] = tiles[k]


def added(a, b):
    return tuple(x + y for x, y in zip(a, b, strict=True))


def split_matrix(back):
    row = lax.broadcasted_iota(jnp.int32, (COLS, COLS), 0)
    column = lax.broadcasted_iota(jnp.int32, (COLS, COLS), 1)
    if back:
        row, column = column, row
    return jnp.where(row == 2 * (column % 128) + column // 128, 1.0, 0.0).astype(BF16)


def permuted(x, matrix):
    high = x.astype(BF16)
    rest = x - high.astype(F32)
    middle = rest.astype(BF16)
    low = (rest - middle.astype(F32)).astype(BF16)
    dot = functools.partial(jnp.dot, preferred_element_type=F32)
    return (dot(high, matrix) + dot(middle, matrix)) + dot(low, matrix)


def prepare_kernel(states, out):
    both = jnp.concatenate([states[0, 0], states[0, 1]], 0)
    moved = permuted(both, split_matrix(False))
    for part in range(PARTS):
        rows = moved[16 * (part % 2) : 16 * (part % 2) + 16]
        for j in range(2):
            out[part, pl.ds(j, 16, stride=2), :] = rows[:, 128 * j : 128 * j + 128]


def read_levels(tables, levels, stage):
    matrix = split_matrix(False)
    for n, table in enumerate(range(3)):
        moved = jnp.dot(tables[table].astype(F32).astype(BF16), matrix, preferred_element_type=F32)
        for j in range(2):
            stage[pl.ds(j, ROWS, stride=2), :] = moved[:, 128 * j : 128 * j + 128]
        store_tiles(levels, load_flat(stage), n)


def steps_of(levels, factor, out):
    five_point(levels, lax.rem(lax.axis_index("space"), 2), factor, out[0])
    for n in range(len(out) - 1):
        compose(out[0], out[n], n + 1, out[n + 1])


def fine_interval(fields, fine2):
    return lax.fori_loop(0, STEPS // 2, lambda _, now: tuple(apply(field, fine2, 2) for field in now), fields)


def coarse_steps(tiles, count, coarse, planes, end=PLANES):
    plane = lax.axis_index("z")
    turns = jnp.where((plane >= planes) & (plane < end), count // 21, 0)

    def body(_, now):
        for _ in range(7):
            now = apply(now, coarse[2], 3)
        return now

    tiles = lax.fori_loop(0, turns, body, tiles)
    count -= count // 21 * 21
    return apply(tiles, coarse[count % 3 - 1], count % 3) if count % 3 else tiles


def coarse_interval(tiles, coarse):
    return apply(apply(apply(tiles, coarse[2], 3), coarse[2], 3), coarse[1], 2)


def where_me():
    return lax.axis_index("z") * PLACES + lax.axis_index("place")


def force(tiles, first, fine2, coarse):
    def body(_, fields):
        ahead, image = fields
        return apply(apply(ahead, fine2, 2), fine2, 2), apply(image, coarse[1], 2)

    ahead, image = lax.fori_loop(0, STEPS // 4, body, (tiles, tiles))
    return ahead, tuple(jnp.where(first, a, a - i) for a, i in zip(ahead, image, strict=True))


def own_kernel(whole, tables, fine2, coarse1, coarse2, coarse3, carried, forcing, stage, levels, fine1):
    read_levels(tables, levels, stage)
    steps_of(levels, 1.0, (fine1, fine2))
    steps_of(levels, 2.0, (coarse1, coarse2, coarse3))
    ahead, forced = force(load_flat(whole), where_me() == 0, fine2, (coarse1, coarse2))
    store_tiles(carried, ahead)
    store_tiles(forcing, forced)


def pair_kernel(behind, forcing, fine2, coarse1, coarse2, coarse3, before, pair):
    coarse = (coarse1, coarse2, coarse3)
    _, forced = force(load_flat(behind), where_me() == PLACES, fine2, coarse)
    store_tiles(before, forced)
    store_tiles(pair, added(coarse_steps(forced, 64, coarse, 1, PLANES - 2), load_tiles(forcing)))


def far_kernel(sixth, coarse1, coarse2, coarse3, out):
    store_tiles(out, coarse_steps(load_tiles(sixth), 128, (coarse1, coarse2, coarse3), 6))


def near_kernel(far, fourth, coarse1, coarse2, coarse3, out):
    total = added(load_tiles(far), load_tiles(fourth))
    store_tiles(out, coarse_steps(total, 128, (coarse1, coarse2, coarse3), 4))


def planes_kernel(near, second, before, forcing, whole, last, ahead, coarse1, coarse2, coarse3, out, gap, past, earlier):
    place, coarse = lax.axis_index("place"), (coarse1, coarse2, coarse3)
    total = added(load_tiles(near), load_tiles(second))
    store_tiles(earlier, total)
    total = added(coarse_steps(total, 64, coarse, 2), load_tiles(before))
    store_tiles(past, total)
    total = added(coarse_steps(total, 64, coarse, 1), load_tiles(forcing))
    store_tiles(gap, tuple(a - b for a, b in zip(load_tiles(ahead), load_flat(last), strict=True)))
    start = load_flat(whole)
    for target in range(PLACES):
        for k in range(TILES):
            value = jnp.where(place <= target - 2, total[k], past[k])
            if target == 0:
                value = jnp.where(place == PLACES - 1, earlier[k], value)
            if target == 1:
                value = jnp.where(where_me() == 0, start[k], value)
            out[target, k] = value


def finish_kernel(sums, gap, carried, fine2, coarse2, coarse3, give, keep, corrected, stage):
    place, part, me = lax.axis_index("place"), lax.axis_index("space"), where_me()
    coarse = (None, coarse2, coarse3)

    def neighbour(k, tiles):
        return added(coarse_interval(tiles, coarse), load_tiles(sums, lax.rem(place + 7 + k, PLACES)))

    total = lax.fori_loop(1, PLACES, neighbour, load_tiles(sums, lax.rem(place + 7, PLACES)))
    total = tuple(jnp.where(me == 1, sums[0, k], t) for k, t in enumerate(total))
    (total,) = fine_interval((total,), fine2)
    store_tiles(corrected, total)
    advanced, residual = fine_interval((total, load_tiles(gap)), fine2)
    advanced = tuple(jnp.where(me == 0, c, a) for c, a in zip(load_tiles(carried), advanced, strict=True))
    other = part + 1 - 2 * lax.rem(part, 2)
    for n, tiles in enumerate((load_tiles(corrected), advanced, residual)):
        store_flat(stage, tiles)
        give[pl.ds(32 * n, 32), :] = stage[pl.ds(pl.multiple_of(32 * other, 32), 32), :]
        keep[pl.ds(32 * n, 32), :] = stage[pl.ds(pl.multiple_of(32 * part, 32), 32), :]


def assemble_kernel(got, kept, states, corrected, advanced, residual):
    interval, own = where_me(), lax.rem(lax.axis_index("space"), 2)
    blocks = []
    for tracer in range(2):
        for n in range(3):
            halves = []
            for j in range(2):
                rows = pl.ds(32 * n + j, 16, stride=2)
                halves.append(jnp.where(own == tracer, kept[rows, :], got[rows, :]))
            blocks.append(jnp.concatenate(halves, 1))
    moved = permuted(jnp.concatenate(blocks, 0), split_matrix(True))
    for tracer in range(2):
        c, a, r = (moved[16 * (3 * tracer + n) : 16 * (3 * tracer + n) + 16] for n in range(3))
        corrected[0, tracer] = jnp.where(interval == 0, states[0, tracer], c)
        advanced[0, tracer] = a
        residual[0, tracer] = jnp.where(interval <= 1, 0.0, r)


def call(kernel, out_shapes, scratch, operands, flops):
    shapes = [jax.ShapeDtypeStruct(shape, F32) for shape in out_shapes]
    moved = 4 * sum(int(np.prod(x.shape)) for x in [*shapes, *operands])
    return pl.pallas_call(
        kernel,
        out_shape=shapes,
        in_specs=[VMEM] * len(operands),
        out_specs=[VMEM] * len(shapes),
        scratch_shapes=scratch,
        compiler_params=pltpu.CompilerParams(vmem_limit_bytes=24 * 2**20),
        cost_estimate=pl.CostEstimate(flops=flops, bytes_accessed=moved, transcendentals=0),
    )(*operands)


def on_device(states, vel_x, vel_y, diffus):
    field, axes = (TILES, 8, 128), ("z", "place")

    def onward(value, steps):
        return lax.ppermute(value, axes, [(i, i + steps) for i in range(INTERVALS - steps)])

    (pieces,) = call(prepare_kernel, [(PARTS, 32, 128)], [], [states], 10**6)
    whole = lax.all_to_all(pieces, "space", 0, 0, tiled=True).reshape(128, 128)
    behind = onward(whole, PLACES)
    stage = pltpu.VMEM((128, 128), F32)
    fine2, coarse1, coarse2, coarse3, carried, forcing = call(
        own_kernel,
        [(len(diamond(radius)), *field) for radius in (2, 1, 2, 3)] + [field, field],
        [stage, pltpu.VMEM((3, *field), F32), coef_scratch(1)],
        [whole, jnp.stack([vel_x, vel_y, diffus])],
        10**7,
    )
    coarse = [coarse1, coarse2, coarse3]
    before, pair = call(pair_kernel, [field, field], [], [behind, forcing, fine2, *coarse], 3 * 10**7)
    sixth, fourth, second = (onward(pair, planes * PLACES) for planes in (6, 4, 2))
    last, ahead = onward(whole, 1), onward(carried, 2)
    (far,) = call(far_kernel, [field], [], [sixth, *coarse], 5 * 10**7)
    (near,) = call(near_kernel, [field], [], [far, fourth, *coarse], 5 * 10**7)
    sums, gap = call(
        planes_kernel,
        [(PLACES, *field), field],
        [pltpu.VMEM(field, F32), pltpu.VMEM(field, F32)],
        [near, second, before, forcing, whole, last, ahead, *coarse],
        5 * 10**7,
    )
    sums = lax.all_to_all(sums, "place", 0, 0, tiled=True)
    give, keep = call(
        finish_kernel,
        [(96, 128), (96, 128)],
        [pltpu.VMEM(field, F32), stage],
        [sums, gap, carried, fine2, coarse2, coarse3],
        3 * 10**7,
    )
    got = lax.ppermute(give, "space", [(part, part ^ 1) for part in range(PARTS)])
    return tuple(call(assemble_kernel, [(1, 2, 16, COLS)] * 3, [], [got, keep, states], 10**7))


def solution(mesh):
    grid = Mesh(mesh.devices.reshape(PLANES, PLACES, PARTS), ("z", "place", "space"))
    split = P(("z", "place"), None, "space", None)
    return jax.shard_map(
        on_device,
        mesh=grid,
        in_specs=(split, P(), P(), P()),
        out_specs=(split, split, split),
        check_vma=False,
    )
```
